128 devices in a mesh: req: 32 (over y, z_hi, x), ctx: 4 (over z_lo, core).
Axes of the slice: x: 4, y: 4, z: 4 (z_hi: 2, z_lo: 2; z = z_hi * 2 + z_lo), core: 2. Of those that a mesh axis runs over, the one named last changes fastest.
Arguments:
- queries: bfloat16 [65536, 2048], P(('req', 'ctx')), may hold values from -2.5 to 2.5, as said below
- keys: bfloat16 [65536, 2048], P(('req', 'ctx')), may hold values from -2.5 to 2.5
- values: bfloat16 [65536, 2048], P(('req', 'ctx')), may hold values from -6 to 6
- residual_in: bfloat16 [65536, 4096], P(('req', 'ctx')), may hold values from -4 to 4
- out_weight: bfloat16 [2048, 4096], P('req', 'ctx'), may hold values from -0.75 to 0.75
- lengths: int32 [32], P('req'), may hold values from 256 to 2048
- routes: int32 [4096, 1], P(('req', 'ctx')), may hold values from 0 to 31; in each aligned block of 32 rows (0 to 31, 32 to 63, ...) at most 2 rows name the same one
Outputs:
- memory: bfloat16 [131072, 4096], P(('req', 'ctx'))
The draws below stay inside these ranges and needn't reach their ends.
Inputs may be any that keep to these rules, and one draw needn't show every extreme that they name: `queries`: hidden draw: some query rows are a multiple of the key row of the same position. `routes`: among the 32 row blocks of one request's position shard, no target appears more than 2 times; in every draw some shard names one target exactly 2 times.
All inputs are finite; a program needn't handle non-finite values.
Results may differ from the reference program's by a relative error of at most 0.012.
Values may be sent and summed in bfloat16 or wider, within the bound.
No kernel may reach another device: no remote copies, remote signals or barrier semaphores. Data moves between devices by JAX's collectives and lax.ppermute only.
A program may use at most 192 MiB of HBM per device.

```python
import math
import jax
import jax.numpy as jnp
import numpy as np
from jax import lax

D = 4096
HEAD_DIM = 256
HEADS = 8
CAP = 2
HF = 2048
SEQ = 2048
REQS = 32
TOKENS = 65536
RB = 16
BLOCKS = 4096
N_REQ = 32
N_CTX = 4


def draw_queries(key, part):
    key = jax.random.fold_in(key, 7)
    base = jnp.clip(0.3 * jax.random.normal(key, (TOKENS, HF)), -2.5, 2.5)
    return base.astype(jnp.bfloat16)


def draw_keys(key, part):
    key = jax.random.fold_in(key, 11)
    base = jnp.clip(0.3 * jax.random.normal(key, (TOKENS, HF)), -2.5, 2.5)
    return base.astype(jnp.bfloat16)


def plant(array, key, least, largest):
    longest = array.shape.index(max(array.shape))
    spots = []
    for shift in (0, 1):
        where = [jax.random.randint(jax.random.fold_in(key, axis), (), 0, length) for axis, length in enumerate(array.shape)]
        where[longest] = (where[longest] + shift) % array.shape[longest]
        spots.append(tuple(where))
    return array.at[spots[0]].set(least).at[spots[1]].set(largest)


def level_of(own_key, dims, shards, smallest, high):
    level = 1.0
    for position, parts in shards:
        steps = jax.random.uniform(jax.random.fold_in(jax.random.fold_in(own_key, 6), position), (parts,), jnp.float32, smallest / len(shards), high / len(shards))
        level = level * jnp.repeat(jnp.exp(steps), dims[position] // parts).reshape((-1,) + (1,) * (len(dims) - 1 - position))
    return level


def routed_block(stream_key, own, number, rows, number_of, top, reach, skew):
    ranking = jax.random.permutation(stream_key, number_of)
    heavy_load, ordinary = shares(number_of, rows * top, reach, skew, True), shares(number_of, rows * top, reach, skew, False)
    places = jnp.arange(number_of)

    def named(tallies, offset_by):
        used = int((tallies > 0).sum())
        fixed = max(1, used // 4)
        shifted = fixed + (places - fixed + offset_by * (used - fixed)) % max(1, number_of - fixed)
        return jnp.zeros((number_of,), jnp.int32).at[ranking[jnp.where(places < fixed, places, shifted)]].set(jnp.asarray(tallies, jnp.int32))

    tallies = jnp.where(number % 4 == 0, named(heavy_load, number // 4), named(ordinary, number - number // 4 - 1))
    mixed = jax.random.permutation(jax.random.fold_in(own, 3), number_of)
    source_of, receiver = mixed[0:number_of // 2 * 2:2], mixed[1:number_of // 2 * 2:2]
    room = jnp.minimum(tallies[source_of] - 1, reach - tallies[receiver]) // 2
    room = jnp.where((source_of == ranking[0]) | (receiver == ranking[0]) | (tallies[receiver] == 0), 0, jnp.maximum(room, 0))
    shifted = jax.random.randint(jax.random.fold_in(own, 4), (number_of // 2,), 0, 1 << 20) % (room + 1)
    tallies = tallies.at[source_of].add(-shifted).at[receiver].add(shifted)
    members = jnp.searchsorted(jnp.cumsum(tallies), jnp.arange(rows * top), side="right").astype(jnp.int32)
    grid = members.reshape(top, rows).T
    grid = grid[jax.random.permutation(jax.random.fold_in(own, 1), rows)]
    offset_by = jax.random.randint(jax.random.fold_in(own, 2), (rows, 1), 0, top)
    return jnp.take_along_axis(grid, (jnp.arange(top)[None, :] + offset_by) % top, axis=1)


def shares(count, total, most, lean, full):
    weights = [(1 << 20) // math.isqrt(grade ** lean) + 1 for grade in range(1, count + 1)]
    largest = most if full else min(most, max(-(-total // count), total * weights[0] // sum(weights)))
    least = 1 if total - largest >= count - 1 else 0
    counts, rest = [largest] + [least] * (count - 1), total - largest - least * (count - 1)
    while rest > 0:
        movable = [i for i in range(1, count) if counts[i] < largest] or [i for i in range(1, count) if counts[i] < most]
        pool, remaining = sum([weights[i] for i in movable]), rest
        for i in movable:
            addition = min(most - counts[i], max(1, remaining * weights[i] // pool), rest)
            counts[i] = counts[i] + addition
            rest = rest - addition
    return np.array(counts)


def scatter_about(stream_key, shape, scale, reach, pieces=(), held_as=jnp.bfloat16):
    entries = jax.random.normal(stream_key, shape, jnp.float32) * scale
    if len(pieces) > 0:
        entries = level_of(stream_key, shape, pieces, -0.22, 0.18) * entries
    return jnp.clip(entries, min=-reach, max=reach).astype(held_as)


def setup_inputs(seed: int = 0) -> dict:
    splits = jax.random.split(jax.random.key(seed), 8)
    queries = draw_queries(jax.random.fold_in(splits[7], 71), 0)
    keys = draw_keys(jax.random.fold_in(splits[7], 71), 0)
    values = scatter_about(splits[2], (TOKENS, HF), 1.0, 6.0, ((0, 128),))
    residual_in = scatter_about(splits[3], (TOKENS, D), 0.5, 4.0, ((0, 128),))
    out_weight = scatter_about(splits[4], (HF, D), (HF // 32) ** -0.5, 0.75, ((0, 32), (1, 4)))
    lengths = plant(jax.random.randint(splits[5], (REQS,), SEQ // 8, SEQ + 1), jax.random.fold_in(splits[5], 1), SEQ // 8, SEQ).astype(jnp.int32)
    routes_keys = jax.random.split(jax.random.fold_in(splits[6], 1), BLOCKS // N_REQ)
    routes_turns = jax.random.permutation(jax.random.fold_in(splits[6], 3), BLOCKS // N_REQ)
    routes = jax.vmap(lambda own, number: routed_block(jax.random.fold_in(splits[6], 2), own, number, N_REQ, N_REQ, 1, CAP, 2))(routes_keys, routes_turns).reshape((BLOCKS, 1))
    return {"queries": queries, "keys": keys, "values": values, "residual_in": residual_in, "out_weight": out_weight, "lengths": lengths, "routes": routes}


NEG_FILL = -1e30


def reference(queries, keys, values, residual_in, out_weight, lengths, routes):
    query_all = queries.reshape(REQS, SEQ, HEADS, HEAD_DIM)
    key_all = keys.reshape(REQS, SEQ, HEADS, HEAD_DIM)
    value_all = values.reshape(REQS, SEQ, HEADS, HEAD_DIM)
    query_block = min(512, SEQ)

    def one_request(request_item):
        query_req, key_req, value_req, length = request_item
        key_float = key_req.astype(jnp.float32)
        value_float = value_req.astype(jnp.float32)
        valid = jnp.arange(SEQ, dtype=jnp.int32) < length

        def one_block(query_rows):
            scores = jnp.einsum("qhe,khe->qhk", query_rows.astype(jnp.float32), key_float)
            scores = jnp.where(valid[None, None, :], scores, NEG_FILL)
            top = jnp.max(scores, axis=2, keepdims=True)
            weights = jnp.where(valid[None, None, :], jnp.exp(scores - top), 0.0)
            total = jnp.sum(weights, axis=2)
            rounded = lax.optimization_barrier(weights.astype(jnp.bfloat16))
            summed = jnp.einsum("qhk,khe->qhe", rounded.astype(jnp.float32), value_float)
            return (summed / total[:, :, None]).astype(jnp.bfloat16)

        blocks = lax.map(one_block, query_req.reshape(SEQ // query_block, query_block, HEADS, HEAD_DIM))
        return blocks.reshape(SEQ, HF)

    attended = lax.map(one_request, (query_all, key_all, value_all, lengths)).reshape(TOKENS, HF)
    encoded = (residual_in.astype(jnp.float32) + jnp.dot(attended, out_weight, preferred_element_type=jnp.float32)).astype(jnp.bfloat16)
    target = routes[:, 0].reshape(REQS, N_CTX, N_REQ)
    choose = (target[:, :, :, None] == jnp.arange(N_REQ, dtype=jnp.int32)[None, None, None, :]).astype(jnp.int32)
    slot_index = jnp.sum((jnp.cumsum(choose, axis=2) - choose) * choose, axis=3)
    request_ids = jnp.arange(REQS, dtype=jnp.int32)[:, None, None]
    shard_ids = jnp.arange(N_CTX, dtype=jnp.int32)[None, :, None]
    places = ((target * N_CTX + shard_ids) * N_REQ + request_ids) * CAP + slot_index
    memory = jnp.zeros((TOKENS * CAP // RB, RB, D), jnp.bfloat16)
    memory = memory.at[places.reshape(-1).astype(jnp.int32)].set(encoded.reshape(BLOCKS, RB, D))
    return memory.reshape(TOKENS * CAP, D)
```

```python
import functools

import jax
import jax.numpy as jnp
from jax import lax
from jax.experimental import pallas as pl
from jax.experimental.pallas import tpu as pltpu
from jax.sharding import PartitionSpec as P

HEAD_DIM = 256
CAP = 2
NEG_FILL = -1e30
CHUNKS = (4, 3, 1)
Q_TILE = 256
COL_TILE = 512
MIB = 1024 * 1024


def flip(x, req_bits, ctx_bits):
    req, ctx = lax.axis_size("req"), lax.axis_size("ctx")
    pairs = [
        (r * ctx + c, (r ^ req_bits) * ctx + (c ^ ctx_bits))
        for r in range(req)
        for c in range(ctx)
    ]
    return lax.ppermute(x, ("req", "ctx"), pairs)


def attend_kernel(meta, q, k0, v0, k1, v1, k2, v2, k3, v3, *rest):
    out = rest[-1]
    rows = q.shape[0]
    count = k0.shape[0]
    keys = (k0, k1, k2, k3)
    vals = (v0, v1, v2, v3)
    biases = []
    for i in range(4):
        at = meta[1 + i] + lax.broadcasted_iota(jnp.int32, (1, count), 1)
        biases.append(jnp.where(at < meta[0], 0.0, NEG_FILL).astype(jnp.float32))
    for tile in range(rows // Q_TILE):
        span = slice(tile * Q_TILE, (tile + 1) * Q_TILE)
        rows_q = q[span, :]
        scores = [
            lax.dot_general(
                rows_q,
                keys[i][...],
                (((1,), (1,)), ((), ())),
                preferred_element_type=jnp.float32,
            )
            + biases[i]
            for i in range(4)
        ]
        top = functools.reduce(
            jnp.maximum, [jnp.max(s, axis=1, keepdims=True) for s in scores]
        )
        total = jnp.zeros((Q_TILE, 1), jnp.float32)
        summed = jnp.zeros((Q_TILE, HEAD_DIM), jnp.float32)
        for i in range(4):
            weights = jnp.exp(scores[i] - top)
            total = total + jnp.sum(weights, axis=1, keepdims=True)
            summed = summed + jnp.dot(
                weights.astype(jnp.bfloat16),
                vals[i][...],
                preferred_element_type=jnp.float32,
            )
        out[span, :] = (summed / total).astype(jnp.bfloat16)


def attend(meta, queries, own, beside, far, far_beside, first, heads, before):
    rows = queries.shape[0]
    count = own[0].shape[0]

    def whole(g, meta):
        return (0, first + g)

    def key_of(g, meta):
        return (0, g)

    def value_of(g, meta):
        return (0, heads + g)

    block = lambda n, index: pl.BlockSpec((n, HEAD_DIM), index)
    return pl.pallas_call(
        attend_kernel,
        grid_spec=pltpu.PrefetchScalarGridSpec(
            num_scalar_prefetch=1,
            grid=(heads,),
            in_specs=[block(rows, whole)]
            + [block(count, whole)] * 4
            + [block(count, key_of), block(count, value_of)] * 2
            + [pl.BlockSpec(memory_space=pl.ANY)] * len(before),
            out_specs=block(rows, whole),
        ),
        out_shape=jax.ShapeDtypeStruct(queries.shape, jnp.bfloat16),
        input_output_aliases={10: 0} if before else {},
        compiler_params=pltpu.CompilerParams(vmem_limit_bytes=32 * MIB),
        cost_estimate=pl.CostEstimate(
            flops=0, bytes_accessed=0, transcendentals=0
        ),
    )(meta, queries, *own, *beside, far, far, far_beside, far_beside, *before)


def project_kernel(place, att, source, residual, out, weight):
    core = pl.program_id(2)
    rows = att.shape[0]
    part = source.shape[0] // 64
    for y in range(4):
        for high in range(2):
            for x in range(4):
                to = ((y * 2 + high) * 4 + x) * part
                fro = pl.multiple_of((((y * 4 + x) * 2 + core) * 2 + high) * part, part)
                weight[to : to + part, :] = source[pl.ds(fro, part), :]
    product = jnp.dot(att[...], weight[...], preferred_element_type=jnp.float32)
    encoded = (residual[...].astype(jnp.float32) + product).astype(jnp.bfloat16)
    out[...] = jnp.zeros(out.shape, jnp.bfloat16)
    blocks = place.shape[0]
    block_rows = rows // blocks
    for i in range(blocks):
        to = pl.multiple_of(place[i] * block_rows, block_rows)
        out[pl.ds(to, block_rows), :] = encoded[i * block_rows : (i + 1) * block_rows]


def project(place, attended, weights, residual):
    rows, width = residual.shape
    depth = attended.shape[1]
    tiles = width // 4 // COL_TILE

    def column(low, t, core, place):
        return (0, (low * 2 + core) * tiles + t)

    return pl.pallas_call(
        project_kernel,
        grid_spec=pltpu.PrefetchScalarGridSpec(
            num_scalar_prefetch=1,
            grid=(2, tiles, 2),
            in_specs=[
                pl.BlockSpec(attended.shape, lambda low, t, core, place: (0, 0)),
                pl.BlockSpec(
                    (2 * depth, COL_TILE),
                    lambda low, t, core, place: (0, low * tiles + t),
                ),
                pl.BlockSpec((rows, COL_TILE), column),
            ],
            out_specs=pl.BlockSpec((CAP * rows, COL_TILE), column),
            scratch_shapes=[pltpu.VMEM((depth, COL_TILE), jnp.bfloat16)],
        ),
        out_shape=jax.ShapeDtypeStruct((CAP * rows, width), jnp.bfloat16),
        compiler_params=pltpu.CompilerParams(vmem_limit_bytes=48 * MIB),
        cost_estimate=pl.CostEstimate(
            flops=2 * rows * depth * width,
            bytes_accessed=2 * depth * width + 6 * rows * width,
            transcendentals=0,
        ),
    )(place, attended, weights, residual)


def shards(queries, keys, values, residual_in, out_weight, lengths, routes):
    req, ctx = lax.axis_index("req"), lax.axis_index("ctx")
    low = ctx // 2
    high = lax.rem(req // 4, 2)
    rows = queries.shape[0]
    req_count = lax.axis_size("req")

    packed = []
    first = 0
    for heads in CHUNKS:
        span = slice(first * HEAD_DIM, (first + heads) * HEAD_DIM)
        packed.append(jnp.concatenate([keys[:, span], values[:, span]], axis=1))
        first += heads
    packed[0], out_weight = lax.optimization_barrier((packed[0], out_weight))

    across = flip(out_weight, 0, 2)
    columns = jnp.where(
        low == 0,
        jnp.concatenate([out_weight, across], axis=1),
        jnp.concatenate([across, out_weight], axis=1),
    )
    above = flip(columns, 4, 0)
    pair = jnp.where(
        high == 0,
        jnp.concatenate([columns, above], axis=0),
        jnp.concatenate([above, columns], axis=0),
    )
    planes = [
        [(y * 8 + h * 4 + x) * 4 + z * 2 + k for y in range(4) for x in range(4) for k in range(2)]
        for h in range(2)
        for z in range(2)
    ]
    weights = lax.all_gather(
        pair, ("req", "ctx"), axis=0, tiled=True, axis_index_groups=planes
    )

    beside = (flip(keys, 0, 1), flip(values, 0, 1))
    positions = jnp.stack([(ctx ^ i) * rows for i in range(4)]).astype(jnp.int32)
    meta = jnp.concatenate([lengths, positions])
    attended = ()
    first = 0
    for i, heads in enumerate(CHUNKS):
        far = flip(packed[i], 0, 2)
        if attended:
            far, *attended = lax.optimization_barrier((far, *attended))
        else:
            far, *packed = lax.optimization_barrier((far, *packed))
        far_beside = flip(far, 0, 1)
        done = attend(
            meta, queries, (keys, values), beside, far, far_beside, first, heads, attended
        )
        attended = (done,)
        first += heads

    target = routes[:, 0]
    blocks = target.shape[0]
    order = jnp.arange(blocks, dtype=jnp.int32)
    same = (target[:, None] == target[None, :]) & (order[None, :] < order[:, None])
    cell = target * CAP + jnp.sum(same.astype(jnp.int32), axis=1)

    placed = project(cell, attended[0], weights, residual_in)
    width = placed.shape[1]
    arrived = lax.all_to_all(
        placed.reshape(req_count, -1, width), "req", split_axis=0, concat_axis=0, tiled=True
    )
    return arrived.reshape(-1, width)


def solution(mesh):
    return jax.shard_map(
        shards,
        mesh=mesh,
        in_specs=(
            P(("req", "ctx"), None),
            P(("req", "ctx"), None),
            P(("req", "ctx"), None),
            P(("req", "ctx"), None),
            P("req", "ctx"),
            P("req"),
            P(("req", "ctx"), None),
        ),
        out_specs=P(("req", "ctx"), None),
        check_vma=False,
    )
```

```python
import functools

import jax
import jax.numpy as jnp
from jax import lax
from jax.experimental import pallas as pl
from jax.experimental.pallas import tpu as pltpu
from jax.sharding import PartitionSpec as P

HEAD_DIM = 256
CAP = 2
NEG_FILL = -1e30
CHUNKS = (1, 4, 2, 1)
Q_TILE = 256
COL_TILE = 512
ROW_TILE = 512
SLOTS = 3
MIB = 1024 * 1024


def flip(x, req_bits, ctx_bits):
    req, ctx = lax.axis_size("req"), lax.axis_size("ctx")
    pairs = [
        (r * ctx + c, (r ^ req_bits) * ctx + (c ^ ctx_bits))
        for r in range(req)
        for c in range(ctx)
    ]
    return lax.ppermute(x, ("req", "ctx"), pairs)


def attend_head(meta, q, keys, vals, out):
    count = keys[0].shape[0]
    biases = []
    for i in range(4):
        at = meta[1 + i] + lax.broadcasted_iota(jnp.int32, (1, count), 1)
        biases.append(jnp.where(at < meta[0], 0.0, NEG_FILL).astype(jnp.float32))
    for tile in range(q.shape[0] // Q_TILE):
        span = slice(tile * Q_TILE, (tile + 1) * Q_TILE)
        rows_q = q[span, :]
        scores = [
            lax.dot_general(
                rows_q,
                keys[i][...],
                (((1,), (1,)), ((), ())),
                preferred_element_type=jnp.float32,
            )
            + biases[i]
            for i in range(4)
        ]
        top = functools.reduce(
            jnp.maximum, [jnp.max(s, axis=1, keepdims=True) for s in scores]
        )
        total = jnp.zeros((Q_TILE, 1), jnp.float32)
        summed = jnp.zeros((Q_TILE, HEAD_DIM), jnp.float32)
        for i in range(4):
            weights = jnp.exp(scores[i] - top)
            total = total + jnp.sum(weights, axis=1, keepdims=True)
            summed = summed + jnp.dot(
                weights.astype(jnp.bfloat16),
                vals[i][...],
                preferred_element_type=jnp.float32,
            )
        out[span, :] = (summed / total).astype(jnp.bfloat16)


def attend_kernel(meta, q, k0, v0, k1, v1, k2, v2, k3, v3, out):
    attend_head(meta, q, (k0, k1, k2, k3), (v0, v1, v2, v3), out)


def attend(meta, queries, own, beside, far, far_beside, first, heads):
    rows = queries.shape[0]
    count = own[0].shape[0]

    def whole(g, meta):
        return (0, first + g)

    def key_of(g, meta):
        return (0, g)

    def value_of(g, meta):
        return (0, heads + g)

    block = lambda n, index: pl.BlockSpec((n, HEAD_DIM), index)
    return pl.pallas_call(
        attend_kernel,
        grid_spec=pltpu.PrefetchScalarGridSpec(
            num_scalar_prefetch=1,
            grid=(heads,),
            in_specs=[block(rows, whole)]
            + [block(count, whole)] * 4
            + [block(count, key_of), block(count, value_of)] * 2,
            out_specs=block(rows, key_of),
        ),
        out_shape=jax.ShapeDtypeStruct((rows, heads * HEAD_DIM), jnp.bfloat16),
        compiler_params=pltpu.CompilerParams(vmem_limit_bytes=20 * MIB),
        cost_estimate=pl.CostEstimate(
            flops=0, bytes_accessed=0, transcendentals=0
        ),
    )(meta, queries, *own, *beside, far, far, far_beside, far_beside)


def finish_kernel(meta, place, q, near, near_beside, far, far_beside, *refs):
    *parts, weights, residual, out, att, held, sems = refs
    step = pl.program_id(0)
    rows, depth = att.shape
    tiles = weights.shape[-1] // 4 // COL_TILE

    def spot(head):
        at = (head % 2 * 4 + head // 2) * HEAD_DIM
        return slice(at, at + HEAD_DIM)

    def fetch(tile, high):
        low, t, core = tile // (2 * tiles), tile // 2 % tiles, tile % 2
        columns = pl.ds(((high * 2 + low) * tiles + t) * COL_TILE, COL_TILE)
        return pltpu.make_async_copy(
            weights.at[:, :, core, :, columns],
            held.at[tile % SLOTS, high],
            sems.at[tile % SLOTS, high],
        )

    @pl.when(step == 0)
    def _():
        for tile in range(SLOTS - 1):
            for high in range(2):
                fetch(tile, high).start()
        half = slice(0, HEAD_DIM), slice(HEAD_DIM, 2 * HEAD_DIM)
        pieces = (near, near_beside, far, far_beside)
        keys = [piece.at[:, half[0]] for piece in pieces]
        vals = [piece.at[:, half[1]] for piece in pieces]
        head = 0
        for part in parts:
            for i in range(part.shape[1] // HEAD_DIM):
                att[:, spot(head)] = part[:, i * HEAD_DIM : (i + 1) * HEAD_DIM]
                head += 1
        attend_head(meta, q, keys, vals, att.at[:, spot(head)])

    for tile in range(4 * tiles):

        @pl.when(step == tile + 1)
        def _():
            for high in range(2):
                fetch(tile, high).wait()
            if tile + SLOTS - 1 < 4 * tiles:
                for high in range(2):
                    fetch(tile + SLOTS - 1, high).start()

    @pl.when(step > 0)
    def _():
        tile = step - 1
        out[...] = jnp.zeros(out.shape, jnp.bfloat16)
        slot = lax.rem(tile, SLOTS)
        lower = held[slot, 0].reshape(depth // 2, COL_TILE)
        upper = held[slot, 1].reshape(depth // 2, COL_TILE)
        blocks = place.shape[0]
        block_rows = rows // blocks
        for part in range(rows // ROW_TILE):
            span = slice(part * ROW_TILE, (part + 1) * ROW_TILE)
            product = jnp.dot(
                att[span, : depth // 2], lower, preferred_element_type=jnp.float32
            ) + jnp.dot(
                att[span, depth // 2 :], upper, preferred_element_type=jnp.float32
            )
            encoded = (residual[span, :].astype(jnp.float32) + product).astype(jnp.bfloat16)
            for i in range(ROW_TILE // block_rows):
                to = place[part * (ROW_TILE // block_rows) + i] * block_rows
                to = pl.multiple_of(to, block_rows)
                out[pl.ds(to, block_rows), :] = encoded[i * block_rows : (i + 1) * block_rows]


def finish(meta, place, query, pieces, attended, weights, residual):
    rows, width = residual.shape
    depth = weights.shape[0]
    tiles = width // 4 // COL_TILE
    part = weights.shape[0] // 32
    weights = weights.reshape(4, 4, 2, part, width)

    def fixed(s, meta, place):
        return (0, 0)

    def column(s, meta, place):
        tile = jnp.maximum(s - 1, 0)
        low, t, core = tile // (2 * tiles), lax.rem(tile // 2, tiles), lax.rem(tile, 2)
        return (0, (low * 2 + core) * tiles + t)

    steps = 4 * tiles
    return pl.pallas_call(
        finish_kernel,
        grid_spec=pltpu.PrefetchScalarGridSpec(
            num_scalar_prefetch=2,
            grid=(steps + 1,),
            in_specs=[pl.BlockSpec(query.shape, fixed)]
            + [pl.BlockSpec(piece.shape, fixed) for piece in (*pieces, *attended)]
            + [
                pl.BlockSpec(memory_space=pl.ANY),
                pl.BlockSpec((rows, COL_TILE), column),
            ],
            out_specs=pl.BlockSpec((CAP * rows, COL_TILE), column),
            scratch_shapes=[
                pltpu.VMEM((rows, depth), jnp.bfloat16),
                pltpu.VMEM((SLOTS, 2, 4, 4, part, COL_TILE), jnp.bfloat16),
                pltpu.SemaphoreType.DMA((SLOTS, 2)),
            ],
        ),
        out_shape=jax.ShapeDtypeStruct((CAP * rows, width), jnp.bfloat16),
        compiler_params=pltpu.CompilerParams(vmem_limit_bytes=28 * MIB),
        cost_estimate=pl.CostEstimate(
            flops=2 * rows * depth * width,
            bytes_accessed=2 * depth * width + 6 * rows * width,
            transcendentals=0,
        ),
    )(meta, place, query, *pieces, *attended, weights, residual)


def hand_over_kernel(arrived, out, sem):
    copy = pltpu.make_async_copy(arrived, out, sem)
    copy.start()
    copy.wait()


def hand_over(arrived):
    return pl.pallas_call(
        hand_over_kernel,
        in_specs=[pl.BlockSpec(memory_space=pltpu.VMEM)],
        out_specs=pl.BlockSpec(memory_space=pl.ANY),
        out_shape=jax.ShapeDtypeStruct(arrived.shape, arrived.dtype),
        scratch_shapes=[pltpu.SemaphoreType.DMA],
        compiler_params=pltpu.CompilerParams(vmem_limit_bytes=12 * MIB),
    )(arrived)


def shards(queries, keys, values, residual_in, out_weight, lengths, routes):
    req, ctx = lax.axis_index("req"), lax.axis_index("ctx")
    low = ctx // 2
    high = lax.rem(req // 4, 2)
    rows = queries.shape[0]
    req_count = lax.axis_size("req")

    packed = []
    first = 0
    for heads in CHUNKS:
        span = slice(first * HEAD_DIM, (first + heads) * HEAD_DIM)
        packed.append(jnp.concatenate([keys[:, span], values[:, span]], axis=1))
        first += heads

    def ordered(bit, mine, other):
        return jnp.where(
            bit == 0,
            jnp.concatenate([mine, other], axis=1),
            jnp.concatenate([other, mine], axis=1),
        )

    pair = ordered(low, out_weight, flip(out_weight, 0, 2))
    aslant = flip(pair, 4, 2)
    nearest = flip(packed[0], 0, 2)
    nearest, pair, aslant, *packed = lax.optimization_barrier(
        (nearest, pair, aslant, *packed)
    )
    pair = ordered(high, pair, aslant)
    planes = [
        [(y * 8 + h * 4 + x) * 4 + z * 2 + k for y in range(4) for x in range(4) for k in range(2)]
        for h in range(2)
        for z in range(2)
    ]
    weights = lax.all_gather(
        pair, ("req", "ctx"), axis=0, tiled=True, axis_index_groups=planes
    )

    beside = (flip(keys, 0, 1), flip(values, 0, 1))
    positions = jnp.stack([(ctx ^ i) * rows for i in range(4)]).astype(jnp.int32)
    meta = jnp.concatenate([lengths, positions])
    attended = ()
    first = 0
    for i, heads in enumerate(CHUNKS):
        far = flip(packed[i], 0, 2) if i else nearest
        if attended:
            far, *attended = lax.optimization_barrier((far, *attended))
        if i == len(CHUNKS) - 2:
            far, weights = lax.optimization_barrier((far, weights))
        far_beside = flip(far, 0, 1)
        if i == len(CHUNKS) - 1:
            break
        done = attend(meta, queries, (keys, values), beside, far, far_beside, first, heads)
        attended = (*attended, done)
        first += heads

    target = routes[:, 0]
    blocks = target.shape[0]
    order = jnp.arange(blocks, dtype=jnp.int32)
    same = (target[:, None] == target[None, :]) & (order[None, :] < order[:, None])
    cell = target * CAP + jnp.sum(same.astype(jnp.int32), axis=1)

    placed = finish(
        meta,
        cell,
        queries[:, first * HEAD_DIM :],
        (packed[-1], flip(packed[-1], 0, 1), far, far_beside),
        attended,
        weights,
        residual_in,
    )
    width = placed.shape[1]
    arrived = lax.all_to_all(
        placed.reshape(req_count, -1, width), "req", split_axis=0, concat_axis=0, tiled=True
    )
    return hand_over(arrived.reshape(-1, width))


def solution(mesh):
    return jax.shard_map(
        shards,
        mesh=mesh,
        in_specs=(
            P(("req", "ctx"), None),
            P(("req", "ctx"), None),
            P(("req", "ctx"), None),
            P(("req", "ctx"), None),
            P("req", "ctx"),
            P("req"),
            P(("req", "ctx"), None),
        ),
        out_specs=P(("req", "ctx"), None),
        check_vma=False,
    )
```

```python
import functools

import jax
import jax.numpy as jnp
from jax import lax
from jax.experimental import pallas as pl
from jax.experimental.pallas import tpu as pltpu
from jax.sharding import PartitionSpec as P

HEAD_DIM = 256
CAP = 2
NEG_FILL = -1e30
CHUNKS = (1, 4, 2, 1)
Q_TILE = 256
COL_TILE = 512
ROW_TILE = 512
SLOTS = 3
MIB = 1024 * 1024


def flip(x, req_bits, ctx_bits):
    req, ctx = lax.axis_size("req"), lax.axis_size("ctx")
    pairs = [
        (r * ctx + c, (r ^ req_bits) * ctx + (c ^ ctx_bits))
        for r in range(req)
        for c in range(ctx)
    ]
    return lax.ppermute(x, ("req", "ctx"), pairs)


def attend_head(meta, q, keys, vals, out):
    count = keys[0].shape[0]
    biases = []
    for i in range(4):
        at = meta[1 + i] + lax.broadcasted_iota(jnp.int32, (1, count), 1)
        biases.append(jnp.where(at < meta[0], 0.0, NEG_FILL).astype(jnp.float32))
    for tile in range(q.shape[0] // Q_TILE):
        span = slice(tile * Q_TILE, (tile + 1) * Q_TILE)
        rows_q = q[span, :]
        scores = [
            lax.dot_general(
                rows_q,
                keys[i][...],
                (((1,), (1,)), ((), ())),
                preferred_element_type=jnp.float32,
            )
            + biases[i]
            for i in range(4)
        ]
        top = functools.reduce(
            jnp.maximum, [jnp.max(s, axis=1, keepdims=True) for s in scores]
        )
        total = jnp.zeros((Q_TILE, 1), jnp.float32)
        summed = jnp.zeros((Q_TILE, HEAD_DIM), jnp.float32)
        for i in range(4):
            weights = jnp.exp(scores[i] - top)
            total = total + jnp.sum(weights, axis=1, keepdims=True)
            summed = summed + jnp.dot(
                weights.astype(jnp.bfloat16),
                vals[i][...],
                preferred_element_type=jnp.float32,
            )
        out[span, :] = (summed / total).astype(jnp.bfloat16)


def attend_kernel(meta, q, k0, v0, k1, v1, k2, v2, k3, v3, out):
    attend_head(meta, q, (k0, k1, k2, k3), (v0, v1, v2, v3), out)


def attend(meta, query, pieces):
    rows, width = query.shape
    heads = width // HEAD_DIM

    def key_of(g, meta):
        return (0, g)

    def value_of(g, meta):
        return (0, heads + g)

    block = lambda index: pl.BlockSpec((rows, HEAD_DIM), index)
    return pl.pallas_call(
        attend_kernel,
        grid_spec=pltpu.PrefetchScalarGridSpec(
            num_scalar_prefetch=1,
            grid=(heads,),
            in_specs=[block(key_of)] + [block(key_of), block(value_of)] * 4,
            out_specs=block(key_of),
        ),
        out_shape=jax.ShapeDtypeStruct(query.shape, jnp.bfloat16),
        compiler_params=pltpu.CompilerParams(vmem_limit_bytes=20 * MIB),
        cost_estimate=pl.CostEstimate(
            flops=0, bytes_accessed=0, transcendentals=0
        ),
    )(meta, query, *[piece for piece in pieces for _ in range(2)])


def finish_kernel(meta, place, q, near, near_beside, far, far_beside, *refs):
    *parts, weights, residual, out, att, held, sems = refs
    step = pl.program_id(0)
    rows, depth = att.shape
    tiles = weights.shape[-1] // 4 // COL_TILE

    def spot(head):
        at = (head % 2 * 4 + head // 2) * HEAD_DIM
        return slice(at, at + HEAD_DIM)

    def fetch(tile, high):
        low, t, core = tile // (2 * tiles), tile // 2 % tiles, tile % 2
        columns = pl.ds(((high * 2 + low) * tiles + t) * COL_TILE, COL_TILE)
        return pltpu.make_async_copy(
            weights.at[:, :, core, :, columns],
            held.at[tile % SLOTS, high],
            sems.at[tile % SLOTS, high],
        )

    @pl.when(step == 0)
    def _():
        for tile in range(SLOTS - 1):
            for high in range(2):
                fetch(tile, high).start()
        half = slice(0, HEAD_DIM), slice(HEAD_DIM, 2 * HEAD_DIM)
        pieces = (near, near_beside, far, far_beside)
        keys = [piece.at[:, half[0]] for piece in pieces]
        vals = [piece.at[:, half[1]] for piece in pieces]
        head = 0
        for part in parts:
            for i in range(part.shape[1] // HEAD_DIM):
                att[:, spot(head)] = part[:, i * HEAD_DIM : (i + 1) * HEAD_DIM]
                head += 1
        attend_head(meta, q, keys, vals, att.at[:, spot(head)])

    for tile in range(4 * tiles):

        @pl.when(step == tile + 1)
        def _():
            for high in range(2):
                fetch(tile, high).wait()
            if tile + SLOTS - 1 < 4 * tiles:
                for high in range(2):
                    fetch(tile + SLOTS - 1, high).start()

    @pl.when(step > 0)
    def _():
        tile = step - 1
        out[...] = jnp.zeros(out.shape, jnp.bfloat16)
        slot = lax.rem(tile, SLOTS)
        lower = held[slot, 0].reshape(depth // 2, COL_TILE)
        upper = held[slot, 1].reshape(depth // 2, COL_TILE)
        blocks = place.shape[0]
        block_rows = rows // blocks
        for part in range(rows // ROW_TILE):
            span = slice(part * ROW_TILE, (part + 1) * ROW_TILE)
            product = jnp.dot(
                att[span, : depth // 2], lower, preferred_element_type=jnp.float32
            ) + jnp.dot(
                att[span, depth // 2 :], upper, preferred_element_type=jnp.float32
            )
            encoded = (residual[span, :].astype(jnp.float32) + product).astype(jnp.bfloat16)
            for i in range(ROW_TILE // block_rows):
                to = place[part * (ROW_TILE // block_rows) + i] * block_rows
                to = pl.multiple_of(to, block_rows)
                out[pl.ds(to, block_rows), :] = encoded[i * block_rows : (i + 1) * block_rows]


def finish(meta, place, query, pieces, attended, weights, residual):
    rows, width = residual.shape
    depth = weights.shape[0]
    tiles = width // 4 // COL_TILE
    part = weights.shape[0] // 32
    weights = weights.reshape(4, 4, 2, part, width)

    def fixed(s, meta, place):
        return (0, 0)

    def column(s, meta, place):
        tile = jnp.maximum(s - 1, 0)
        low, t, core = tile // (2 * tiles), lax.rem(tile // 2, tiles), lax.rem(tile, 2)
        return (0, (low * 2 + core) * tiles + t)

    steps = 4 * tiles
    return pl.pallas_call(
        finish_kernel,
        grid_spec=pltpu.PrefetchScalarGridSpec(
            num_scalar_prefetch=2,
            grid=(steps + 1,),
            in_specs=[pl.BlockSpec(query.shape, fixed)]
            + [pl.BlockSpec(piece.shape, fixed) for piece in (*pieces, *attended)]
            + [
                pl.BlockSpec(memory_space=pl.ANY),
                pl.BlockSpec((rows, COL_TILE), column),
            ],
            out_specs=pl.BlockSpec((CAP * rows, COL_TILE), column),
            scratch_shapes=[
                pltpu.VMEM((rows, depth), jnp.bfloat16),
                pltpu.VMEM((SLOTS, 2, 4, 4, part, COL_TILE), jnp.bfloat16),
                pltpu.SemaphoreType.DMA((SLOTS, 2)),
            ],
        ),
        out_shape=jax.ShapeDtypeStruct((CAP * rows, width), jnp.bfloat16),
        compiler_params=pltpu.CompilerParams(vmem_limit_bytes=28 * MIB),
        cost_estimate=pl.CostEstimate(
            flops=2 * rows * depth * width,
            bytes_accessed=2 * depth * width + 6 * rows * width,
            transcendentals=0,
        ),
    )(meta, place, query, *pieces, *attended, weights, residual)


def hand_over_kernel(arrived, out, sem):
    copy = pltpu.make_async_copy(arrived, out, sem)
    copy.start()
    copy.wait()


def hand_over(arrived):
    return pl.pallas_call(
        hand_over_kernel,
        in_specs=[pl.BlockSpec(memory_space=pltpu.VMEM)],
        out_specs=pl.BlockSpec(memory_space=pl.ANY),
        out_shape=jax.ShapeDtypeStruct(arrived.shape, arrived.dtype),
        scratch_shapes=[pltpu.SemaphoreType.DMA],
        compiler_params=pltpu.CompilerParams(vmem_limit_bytes=12 * MIB),
    )(arrived)


def shards(queries, keys, values, residual_in, out_weight, lengths, routes):
    req, ctx = lax.axis_index("req"), lax.axis_index("ctx")
    low = ctx // 2
    high = lax.rem(req // 4, 2)
    rows = queries.shape[0]
    req_count = lax.axis_size("req")

    packed = []
    first = 0
    for heads in CHUNKS:
        span = slice(first * HEAD_DIM, (first + heads) * HEAD_DIM)
        packed.append(jnp.concatenate([keys[:, span], values[:, span]], axis=1))
        first += heads

    def ordered(bit, mine, other):
        return jnp.where(
            bit == 0,
            jnp.concatenate([mine, other], axis=1),
            jnp.concatenate([other, mine], axis=1),
        )

    pair = ordered(low, out_weight, flip(out_weight, 0, 2))
    aslant = flip(pair, 4, 2)
    nearest = flip(packed[0], 0, 2)
    nearest, pair, aslant, *_ = lax.optimization_barrier((nearest, pair, aslant, *packed))
    pair = ordered(high, pair, aslant)
    planes = [
        [(y * 8 + h * 4 + x) * 4 + z * 2 + k for y in range(4) for x in range(4) for k in range(2)]
        for h in range(2)
        for z in range(2)
    ]
    weights = lax.all_gather(
        pair, ("req", "ctx"), axis=0, tiled=True, axis_index_groups=planes
    )

    beside = [flip(near, 0, 1) for near in packed]
    positions = jnp.stack([(ctx ^ i) * rows for i in range(4)]).astype(jnp.int32)
    meta = jnp.concatenate([lengths, positions])
    attended = ()
    first = 0
    for i, heads in enumerate(CHUNKS):
        far = flip(packed[i], 0, 2) if i else nearest
        if attended:
            far, *attended = lax.optimization_barrier((far, *attended))
        if i == len(CHUNKS) - 2:
            far, weights = lax.optimization_barrier((far, weights))
        far_beside = flip(far, 0, 1)
        if i == len(CHUNKS) - 1:
            break
        query = queries[:, first * HEAD_DIM : (first + heads) * HEAD_DIM]
        done = attend(meta, query, (packed[i], beside[i], far, far_beside))
        attended = (*attended, done)
        first += heads

    target = routes[:, 0]
    blocks = target.shape[0]
    order = jnp.arange(blocks, dtype=jnp.int32)
    same = (target[:, None] == target[None, :]) & (order[None, :] < order[:, None])
    cell = target * CAP + jnp.sum(same.astype(jnp.int32), axis=1)

    placed = finish(
        meta,
        cell,
        queries[:, first * HEAD_DIM :],
        (packed[-1], beside[-1], far, far_beside),
        attended,
        weights,
        residual_in,
    )
    width = placed.shape[1]
    arrived = lax.all_to_all(
        placed.reshape(req_count, -1, width), "req", split_axis=0, concat_axis=0, tiled=True
    )
    return hand_over(arrived.reshape(-1, width))


def solution(mesh):
    return jax.shard_map(
        shards,
        mesh=mesh,
        in_specs=(
            P(("req", "ctx"), None),
            P(("req", "ctx"), None),
            P(("req", "ctx"), None),
            P(("req", "ctx"), None),
            P("req", "ctx"),
            P("req"),
            P(("req", "ctx"), None),
        ),
        out_specs=P(("req", "ctx"), None),
        check_vma=False,
    )
```

```python
import functools

import jax
import jax.numpy as jnp
from jax import lax
from jax.experimental import pallas as pl
from jax.experimental.pallas import tpu as pltpu
from jax.sharding import PartitionSpec as P

HEAD_DIM = 256
CAP = 2
NEG_FILL = -1e30
CHUNKS = (1, 4, 2, 1)
Q_TILE = 256
COL_TILE = 1024
ROW_TILE = 512
SLOTS = 3
MIB = 1024 * 1024


def flip(x, req_bits, ctx_bits):
    req, ctx = lax.axis_size("req"), lax.axis_size("ctx")
    pairs = [
        (r * ctx + c, (r ^ req_bits) * ctx + (c ^ ctx_bits))
        for r in range(req)
        for c in range(ctx)
    ]
    return lax.ppermute(x, ("req", "ctx"), pairs)


def attend_head(meta, q, keys, vals, out):
    count = keys[0].shape[0]
    biases = []
    for i in range(4):
        at = meta[1 + i] + lax.broadcasted_iota(jnp.int32, (1, count), 1)
        biases.append(jnp.where(at < meta[0], 0.0, NEG_FILL).astype(jnp.float32))
    for tile in range(q.shape[0] // Q_TILE):
        span = slice(tile * Q_TILE, (tile + 1) * Q_TILE)
        rows_q = q[span, :]
        scores = [
            lax.dot_general(
                rows_q,
                keys[i][...],
                (((1,), (1,)), ((), ())),
                preferred_element_type=jnp.float32,
            )
            + biases[i]
            for i in range(4)
        ]
        top = functools.reduce(
            jnp.maximum, [jnp.max(s, axis=1, keepdims=True) for s in scores]
        )
        total = jnp.zeros((Q_TILE, 1), jnp.float32)
        summed = jnp.zeros((Q_TILE, HEAD_DIM), jnp.float32)
        for i in range(4):
            weights = jnp.exp(scores[i] - top)
            total = total + jnp.sum(weights, axis=1, keepdims=True)
            summed = summed + jnp.dot(
                weights.astype(jnp.bfloat16),
                vals[i][...],
                preferred_element_type=jnp.float32,
            )
        out[span, :] = (summed / total).astype(jnp.bfloat16)


def attend_kernel(meta, q, k0, v0, k1, v1, k2, v2, k3, v3, out):
    attend_head(meta, q, (k0, k1, k2, k3), (v0, v1, v2, v3), out)


def attend(meta, query, pieces):
    rows, width = query.shape
    heads = width // HEAD_DIM

    def key_of(g, meta):
        return (0, g)

    def value_of(g, meta):
        return (0, heads + g)

    block = lambda index: pl.BlockSpec((rows, HEAD_DIM), index)
    return pl.pallas_call(
        attend_kernel,
        grid_spec=pltpu.PrefetchScalarGridSpec(
            num_scalar_prefetch=1,
            grid=(heads,),
            in_specs=[block(key_of)] + [block(key_of), block(value_of)] * 4,
            out_specs=block(key_of),
        ),
        out_shape=jax.ShapeDtypeStruct(query.shape, jnp.bfloat16),
        compiler_params=pltpu.CompilerParams(vmem_limit_bytes=20 * MIB),
        cost_estimate=pl.CostEstimate(
            flops=0, bytes_accessed=0, transcendentals=0
        ),
    )(meta, query, *[piece for piece in pieces for _ in range(2)])


def finish_kernel(meta, place, q, near, near_beside, far, far_beside, *refs):
    *parts, weights, residual, out, att, held, sems = refs
    step = pl.program_id(0)
    rows, depth = att.shape
    tiles = weights.shape[-1] // 4 // COL_TILE

    def spot(head):
        at = (head % 2 * 4 + head // 2) * HEAD_DIM
        return slice(at, at + HEAD_DIM)

    def fetch(tile, high):
        low, t, core = tile // (2 * tiles), tile // 2 % tiles, tile % 2
        columns = pl.ds(((high * 2 + low) * tiles + t) * COL_TILE, COL_TILE)
        return pltpu.make_async_copy(
            weights.at[:, :, core, :, columns],
            held.at[tile % SLOTS, high],
            sems.at[tile % SLOTS, high],
        )

    @pl.when(step == 0)
    def _():
        for tile in range(SLOTS - 1):
            for high in range(2):
                fetch(tile, high).start()
        half = slice(0, HEAD_DIM), slice(HEAD_DIM, 2 * HEAD_DIM)
        pieces = (near, near_beside, far, far_beside)
        keys = [piece.at[:, half[0]] for piece in pieces]
        vals = [piece.at[:, half[1]] for piece in pieces]
        head = 0
        for part in parts:
            for i in range(part.shape[1] // HEAD_DIM):
                att[:, spot(head)] = part[:, i * HEAD_DIM : (i + 1) * HEAD_DIM]
                head += 1
        attend_head(meta, q, keys, vals, att.at[:, spot(head)])

    for tile in range(4 * tiles):

        @pl.when(step == tile + 1)
        def _():
            for high in range(2):
                fetch(tile, high).wait()
            if tile + SLOTS - 1 < 4 * tiles:
                for high in range(2):
                    fetch(tile + SLOTS - 1, high).start()

    @pl.when(step > 0)
    def _():
        tile = step - 1
        out[...] = jnp.zeros(out.shape, jnp.bfloat16)
        slot = lax.rem(tile, SLOTS)
        lower = held[slot, 0].reshape(depth // 2, COL_TILE)
        upper = held[slot, 1].reshape(depth // 2, COL_TILE)
        blocks = place.shape[0]
        block_rows = rows // blocks
        for part in range(rows // ROW_TILE):
            span = slice(part * ROW_TILE, (part + 1) * ROW_TILE)
            product = jnp.dot(
                att[span, : depth // 2], lower, preferred_element_type=jnp.float32
            ) + jnp.dot(
                att[span, depth // 2 :], upper, preferred_element_type=jnp.float32
            )
            encoded = (residual[span, :].astype(jnp.float32) + product).astype(jnp.bfloat16)
            for i in range(ROW_TILE // block_rows):
                to = place[part * (ROW_TILE // block_rows) + i] * block_rows
                to = pl.multiple_of(to, block_rows)
                out[pl.ds(to, block_rows), :] = encoded[i * block_rows : (i + 1) * block_rows]


def finish(meta, place, query, pieces, attended, weights, residual):
    rows, width = residual.shape
    depth = weights.shape[0]
    tiles = width // 4 // COL_TILE
    part = weights.shape[0] // 32
    weights = weights.reshape(4, 4, 2, part, width)

    def fixed(s, meta, place):
        return (0, 0)

    def column(s, meta, place):
        tile = jnp.maximum(s - 1, 0)
        low, t, core = tile // (2 * tiles), lax.rem(tile // 2, tiles), lax.rem(tile, 2)
        return (0, (low * 2 + core) * tiles + t)

    steps = 4 * tiles
    return pl.pallas_call(
        finish_kernel,
        grid_spec=pltpu.PrefetchScalarGridSpec(
            num_scalar_prefetch=2,
            grid=(steps + 1,),
            in_specs=[pl.BlockSpec(query.shape, fixed)]
            + [pl.BlockSpec(piece.shape, fixed) for piece in (*pieces, *attended)]
            + [
                pl.BlockSpec(memory_space=pl.ANY),
                pl.BlockSpec((rows, COL_TILE), column),
            ],
            out_specs=pl.BlockSpec((CAP * rows, COL_TILE), column),
            scratch_shapes=[
                pltpu.VMEM((rows, depth), jnp.bfloat16),
                pltpu.VMEM((SLOTS, 2, 4, 4, part, COL_TILE), jnp.bfloat16),
                pltpu.SemaphoreType.DMA((SLOTS, 2)),
            ],
        ),
        out_shape=jax.ShapeDtypeStruct((CAP * rows, width), jnp.bfloat16),
        compiler_params=pltpu.CompilerParams(vmem_limit_bytes=40 * MIB),
        cost_estimate=pl.CostEstimate(
            flops=2 * rows * depth * width,
            bytes_accessed=2 * depth * width + 6 * rows * width,
            transcendentals=0,
        ),
    )(meta, place, query, *pieces, *attended, weights, residual)


def hand_over_kernel(arrived, out, sem):
    copy = pltpu.make_async_copy(arrived, out, sem)
    copy.start()
    copy.wait()


def hand_over(arrived):
    return pl.pallas_call(
        hand_over_kernel,
        in_specs=[pl.BlockSpec(memory_space=pltpu.VMEM)],
        out_specs=pl.BlockSpec(memory_space=pl.ANY),
        out_shape=jax.ShapeDtypeStruct(arrived.shape, arrived.dtype),
        scratch_shapes=[pltpu.SemaphoreType.DMA],
        compiler_params=pltpu.CompilerParams(vmem_limit_bytes=12 * MIB),
    )(arrived)


def shards(queries, keys, values, residual_in, out_weight, lengths, routes):
    req, ctx = lax.axis_index("req"), lax.axis_index("ctx")
    low = ctx // 2
    high = lax.rem(req // 4, 2)
    rows = queries.shape[0]
    req_count = lax.axis_size("req")

    packed = []
    first = 0
    for heads in CHUNKS:
        span = slice(first * HEAD_DIM, (first + heads) * HEAD_DIM)
        packed.append(jnp.concatenate([keys[:, span], values[:, span]], axis=1))
        first += heads

    def ordered(bit, mine, other):
        return jnp.where(
            bit == 0,
            jnp.concatenate([mine, other], axis=1),
            jnp.concatenate([other, mine], axis=1),
        )

    pair = ordered(low, out_weight, flip(out_weight, 0, 2))
    aslant = flip(pair, 4, 2)
    nearest = flip(packed[0], 0, 2)
    nearest, pair, aslant, *_ = lax.optimization_barrier((nearest, pair, aslant, *packed))
    pair = ordered(high, pair, aslant)
    planes = [
        [(y * 8 + h * 4 + x) * 4 + z * 2 + k for y in range(4) for x in range(4) for k in range(2)]
        for h in range(2)
        for z in range(2)
    ]
    weights = lax.all_gather(
        pair, ("req", "ctx"), axis=0, tiled=True, axis_index_groups=planes
    )

    beside = [flip(near, 0, 1) for near in packed]
    positions = jnp.stack([(ctx ^ i) * rows for i in range(4)]).astype(jnp.int32)
    meta = jnp.concatenate([lengths, positions])
    attended = ()
    first = 0
    for i, heads in enumerate(CHUNKS):
        far = flip(packed[i], 0, 2) if i else nearest
        if attended:
            far, *attended = lax.optimization_barrier((far, *attended))
        if i == len(CHUNKS) - 2:
            far, weights = lax.optimization_barrier((far, weights))
        far_beside = flip(far, 0, 1)
        if i == len(CHUNKS) - 1:
            break
        query = queries[:, first * HEAD_DIM : (first + heads) * HEAD_DIM]
        done = attend(meta, query, (packed[i], beside[i], far, far_beside))
        attended = (*attended, done)
        first += heads

    target = routes[:, 0]
    blocks = target.shape[0]
    order = jnp.arange(blocks, dtype=jnp.int32)
    same = (target[:, None] == target[None, :]) & (order[None, :] < order[:, None])
    cell = target * CAP + jnp.sum(same.astype(jnp.int32), axis=1)

    placed = finish(
        meta,
        cell,
        queries[:, first * HEAD_DIM :],
        (packed[-1], beside[-1], far, far_beside),
        attended,
        weights,
        residual_in,
    )
    width = placed.shape[1]
    arrived = lax.all_to_all(
        placed.reshape(req_count, -1, width), "req", split_axis=0, concat_axis=0, tiled=True
    )
    return hand_over(arrived.reshape(-1, width))


def solution(mesh):
    return jax.shard_map(
        shards,
        mesh=mesh,
        in_specs=(
            P(("req", "ctx"), None),
            P(("req", "ctx"), None),
            P(("req", "ctx"), None),
            P(("req", "ctx"), None),
            P("req", "ctx"),
            P("req"),
            P(("req", "ctx"), None),
        ),
        out_specs=P(("req", "ctx"), None),
        check_vma=False,
    )
```
